32 devices in a mesh: parts: 2 (over x), ctx: 16 (over z, y, core).
Axes of the slice: x: 2, y: 2, z: 4, core: 2. Of those that a mesh axis runs over, the one named last changes fastest.
Arguments:
- hidden_states: bfloat16 [8192, 8192], P(('parts', 'ctx')), parts along dimension 0, may hold values from -6 to 6
- queries: bfloat16 [8192, 4096], P(('parts', 'ctx')), parts along dimension 0, may hold values from -360 to 360
- w_key: bfloat16 [8192, 512], P('ctx'), may hold values from -0.0625 to 0.0625
- w_value: bfloat16 [8192, 512], P('ctx'), may hold values from -0.0625 to 0.0625
- doc_ids: int32 [8192], P(('parts', 'ctx')), parts along dimension 0, may hold values from 0 to 7, never falling along the last dimension, each value on 1 to 1024 neighbouring positions
Outputs:
- attended: bfloat16 [8192, 4096], P(('parts', 'ctx')), parts along dimension 0
The draws below stay inside these ranges and needn't reach their ends.
There are 2 independent parts, one for each index of `parts`. The reference program is written for one: setup_inputs(seed, part) draws one part's arguments, and reference() takes and returns one part's arrays. A program takes and returns all parts, laid end to end along the dimension named above; an argument that names none is the same for every part. Nothing has to cross between parts.
Inputs may be any that keep to these rules, and one draw needn't show every extreme that they name: doc_ids never fall along the sequence; each document has 1 to 1024 tokens and one has exactly 1024.
All inputs are finite; a program needn't handle non-finite values.
Results may differ from the reference program's by a relative error of at most 0.004.
The reference program's roundings to bfloat16 on the way count: a program that leaves them out, or rounds other values in their place, can miss the bound.
Values may be sent and summed in bfloat16 or wider, within the bound.
A program may use at most 128 MiB of HBM per device.

```python
import math
import jax
import jax.numpy as jnp
import numpy as np
from jax import lax

D = 8192
HEAD_DIM = 128
HEADS = 32
KV_HEADS = 4
TOK_DEV = 256
DOC_MOST = 1024
TOKENS = 4096
QW = 4096
KVW = 512
N_CTX = 16


def draw_queries(key, part):
    key = jax.random.fold_in(key, 7)
    values_drawn = jnp.clip(jax.random.normal(key, (TOKENS, HEADS * HEAD_DIM), jnp.float32), -6.0, 6.0)
    return values_drawn.astype(jnp.bfloat16)


def steps_of(rng, extent, shards, low, largest):
    def one(dim, shards_of):
        draws = jax.random.uniform(jax.random.fold_in(jax.random.fold_in(rng, 6), dim), (shards_of,), jnp.float32, low / len(shards), largest / len(shards))
        return jnp.repeat(jnp.exp(draws), extent[dim] // shards_of).reshape((-1,) + (1,) * (len(extent) - dim - 1))

    gain = one(*shards[0])
    for cut in shards[1:]:
        gain = gain * one(*cut)
    return gain


def profile(amount, total, reach, skew):
    loads = [(1 << 20) // math.isqrt(rank ** skew) + 1 for rank in range(2, amount + 1)]
    surplus, given = total - reach - (amount - 1), [1] * (amount - 1)
    while surplus > 0:
        free = [i for i in range(amount - 1) if given[i] < reach]
        whole, budget = sum([loads[i] for i in free]), surplus
        for i in free:
            more = min(reach - given[i], max(1, budget * loads[i] // whole), surplus)
            given[i] = given[i] + more
            surplus = surplus - more
    return np.array([reach] + given)


def uneven(key, count, total, reach, skew):
    if count == 2:
        one = jax.random.randint(key, (), max(1, total - reach), min(reach, total - 1) + 1)
        return jnp.stack([one, total - one])
    sizes = jnp.asarray(profile(count, total, reach, skew), jnp.int32)
    pairs = (count - 1) // 2
    source_of, taker = sizes[1:1 + 2 * pairs:2], sizes[2:2 + 2 * pairs:2]
    slack = jnp.minimum(source_of - 1, reach - taker)
    moved = jax.random.randint(jax.random.fold_in(key, 1), (pairs,), 0, 1 << 20) % (slack + 1)
    sizes = sizes.at[1:1 + 2 * pairs:2].set(source_of - moved).at[2:2 + 2 * pairs:2].set(taker + moved)
    return sizes[jax.random.permutation(jax.random.fold_in(key, 2), count)]


def scatter_about(own_key, dims, scale, reach, cuts=(), held_as=jnp.bfloat16):
    entries = scale * jax.random.normal(own_key, dims, jnp.float32)
    if cuts:
        entries = entries * steps_of(own_key, dims, cuts, -0.22, 0.18)
    return jnp.clip(entries, -reach, reach).astype(held_as)


def setup_inputs(seed: int = 0, part: int = 0) -> dict:
    arg_keys = jax.random.split(jax.random.key(seed), 6)
    part_keys = jax.random.split(jax.random.fold_in(arg_keys[5], part), 6)
    return {
        "hidden_states": scatter_about(part_keys[0], (TOKENS, D), 1.0, 6.0, ((0, 16),)),
        "queries": draw_queries(jax.random.fold_in(jax.random.fold_in(arg_keys[5], part), 71), part),
        "w_key": scatter_about(arg_keys[2], (D, KVW), D ** -0.5, 0.0625, ((0, 16),)),
        "w_value": scatter_about(arg_keys[3], (D, KVW), D ** -0.5, 0.0625, ((0, 16),)),
        "doc_ids": jnp.searchsorted(jnp.cumsum(uneven(part_keys[4], N_CTX // 2, TOKENS, DOC_MOST, 1)), jnp.arange(TOKENS), side="right").astype(jnp.int32),
    }


def rotate(key_raw, positions):
    half_dim = HEAD_DIM // 2
    inverse_freq = 500000.0 ** (-jnp.arange(half_dim).astype(jnp.float32) * 2.0 / HEAD_DIM)
    angles = positions.astype(jnp.float32)[:, None] * inverse_freq[None, :]
    cosine = jnp.cos(angles)[:, None, :]
    sine = jnp.sin(angles)[:, None, :]
    shaped = key_raw.reshape(key_raw.shape[0], KV_HEADS, HEAD_DIM)
    first_half = shaped[..., :half_dim]
    second_half = shaped[..., half_dim:]
    turned = jnp.concatenate([first_half * cosine - second_half * sine, second_half * cosine + first_half * sine], -1)
    return turned.reshape(key_raw.shape[0], KVW)

def attend(query_rows, key_rows, value_rows, allowed):
    group_size = HEADS // KV_HEADS
    num_q = query_rows.shape[0]
    num_k = key_rows.shape[0]
    q_heads = query_rows.reshape(num_q, KV_HEADS, group_size, HEAD_DIM).transpose(1, 0, 2, 3)
    k_heads = key_rows.reshape(num_k, KV_HEADS, HEAD_DIM).transpose(1, 0, 2)
    v_heads = value_rows.reshape(num_k, KV_HEADS, HEAD_DIM).transpose(1, 0, 2)

    def one_head(packed):
        q_one, k_one, v_one = packed
        scores = jnp.einsum('bgd,kd->gbk', q_one.astype(jnp.float32), k_one.astype(jnp.float32)) / jnp.sqrt(jnp.float32(HEAD_DIM))
        scores = jnp.where(allowed[None], scores, -jnp.inf)
        row_max = lax.optimization_barrier(jnp.max(scores, -1, keepdims=True))
        expo = jnp.exp(scores - row_max)
        probs = (expo / lax.optimization_barrier(jnp.sum(expo, -1, keepdims=True))).astype(jnp.bfloat16)
        return jnp.einsum('gbk,kd->bgd', probs.astype(jnp.float32), v_one.astype(jnp.float32))
    result = lax.map(one_head, (q_heads, k_heads, v_heads))
    return result.transpose(1, 0, 2, 3).reshape(num_q, HEADS * HEAD_DIM).astype(jnp.bfloat16)

def reference(hidden_states, queries, w_key, w_value, doc_ids):
    hidden_f32 = hidden_states.astype(jnp.float32)
    normed = (hidden_f32 * lax.rsqrt(lax.optimization_barrier(jnp.mean(hidden_f32 * hidden_f32, -1, keepdims=True)) + 1e-05)).astype(jnp.bfloat16)
    positions = jnp.arange(TOKENS).astype(jnp.int32)
    key_raw = jnp.dot(normed, w_key, preferred_element_type=jnp.float32)
    key_all = rotate(key_raw, positions).astype(jnp.bfloat16)
    value_all = jnp.dot(normed, w_value, preferred_element_type=jnp.float32).astype(jnp.bfloat16)
    key_pad = jnp.concatenate([jnp.zeros((DOC_MOST, KVW), jnp.bfloat16), key_all], 0)
    value_pad = jnp.concatenate([jnp.zeros((DOC_MOST, KVW), jnp.bfloat16), value_all], 0)
    doc_pad = jnp.concatenate([jnp.zeros((DOC_MOST,), jnp.int32) - 1, doc_ids.astype(jnp.int32)], 0)
    pos_pad = jnp.arange(-DOC_MOST, TOKENS).astype(jnp.int32)
    span = DOC_MOST + TOK_DEV

    def one_block(block_num):
        first_row = (block_num * TOK_DEV).astype(jnp.int32)
        q_rows = lax.dynamic_slice_in_dim(queries, first_row, TOK_DEV, 0)
        q_docs = lax.dynamic_slice_in_dim(doc_ids.astype(jnp.int32), first_row, TOK_DEV, 0)
        q_pos = first_row + jnp.arange(TOK_DEV).astype(jnp.int32)
        k_rows = lax.dynamic_slice_in_dim(key_pad, first_row, span, 0)
        v_rows = lax.dynamic_slice_in_dim(value_pad, first_row, span, 0)
        k_docs = lax.dynamic_slice_in_dim(doc_pad, first_row, span, 0)
        k_pos = lax.dynamic_slice_in_dim(pos_pad, first_row, span, 0)
        allowed = (k_docs[None, :] == q_docs[:, None]) & (k_pos[None, :] <= q_pos[:, None]) & (k_pos[None, :] >= 0)
        return attend(q_rows, k_rows, v_rows, allowed)
    blocks = lax.map(one_block, jnp.arange(TOKENS // TOK_DEV).astype(jnp.int32))
    return blocks.reshape(TOKENS, QW)
```

```python
import functools
import math

import jax
import jax.numpy as jnp
from jax import lax
from jax.experimental import pallas as pl
from jax.experimental.pallas import tpu as pltpu
from jax.sharding import PartitionSpec as P

HEAD_DIM = 128
HEADS = 32
KV_HEADS = 4
REACH = 4
GROUP = HEADS // KV_HEADS
MESH = pl.DeviceIdType.MESH


def project_kernel(n, parts, hidden, wk, wv, cos2, sin2, doc, kout, vout, dout,
                   w_all, normed, acc, own_sem, ring_s, ring_r, sib_s, sib_r, x_s, x_r,
                   xs_s, xs_r, ex_s, ex_r, doc_s, doc_r):
    chips = n // 2
    rows = wk.shape[0]
    half = rows // 2
    third = (half // 48) * 16 if parts == 2 else 0
    length = half - third
    tok = hidden.shape[0]
    depth = hidden.shape[1]

    idx = lax.axis_index("ctx")
    part = lax.axis_index("parts")
    core = idx % 2
    chip_no = idx // 2
    col = chip_no % 2
    lane = chip_no // 2
    pos = col * (chips - 1 - lane) + (1 - col) * lane
    sibling = idx + 1 - 2 * core

    def chip_at(place):
        upper = place // (chips // 2)
        return (1 - upper) * 2 * place + upper * (2 * (chips - 1 - place) + 1)

    def base(d, s, which_core):
        owner = (pos + chips - s) % chips if d == 0 else (pos + s) % chips
        return (2 * chip_at(owner) + which_core) * rows + d * half

    def at(m, start, count):
        return w_all.at[m, pl.ds(pl.multiple_of(start, 16), count), :]

    def ring(m, d, s, recv_s):
        target = (pos + 1) % chips if d == 0 else (pos + chips - 1) % chips
        piece = at(m, base(d, s, core) + part * third, length)
        return pltpu.make_async_remote_copy(
            piece, piece, ring_s.at[m, d, s], ring_r.at[m, d, recv_s],
            device_id={"ctx": 2 * chip_at(target) + core}, device_id_type=MESH)

    def sib_own(m, d, which_core):
        piece = at(m, base(d, 0, which_core), half)
        return pltpu.make_async_remote_copy(
            piece, piece, sib_s.at[m, d, 0], sib_r.at[m, d, 0],
            device_id={"ctx": sibling}, device_id_type=MESH)

    def sib(m, d, s, which_core):
        piece = at(m, base(d, s, which_core) + part * third, length)
        return pltpu.make_async_remote_copy(
            piece, piece, sib_s.at[m, d, s], sib_r.at[m, d, s],
            device_id={"ctx": sibling}, device_id_type=MESH)

    def cross(m, d, s, of_part):
        piece = at(m, base(d, s, core) + of_part * (half - third), third)
        return pltpu.make_async_remote_copy(
            piece, piece, x_s.at[m, d, s], x_r.at[m, d, s],
            device_id={"parts": 1 - part}, device_id_type=MESH)

    def cross_sib(m, d, s, which_core):
        piece = at(m, base(d, s, which_core) + (1 - part) * (half - third), third)
        return pltpu.make_async_remote_copy(
            piece, piece, xs_s.at[m, d, s], xs_r.at[m, d, s],
            device_id={"ctx": sibling}, device_id_type=MESH)

    def send_docs(o):
        return pltpu.make_async_remote_copy(
            doc, dout.at[o], doc_s.at[o - 1], doc_r.at[o - 1],
            device_id={"ctx": (idx + o) % n}, device_id_type=MESH)

    def send_ahead(m, buf, o):
        return pltpu.make_async_remote_copy(
            buf.at[0], buf.at[o], ex_s.at[m, o - 1], ex_r.at[m, o - 1],
            device_id={"ctx": (idx + o) % n}, device_id_type=MESH)

    def send_beside(m, buf, o):
        return pltpu.make_async_remote_copy(
            buf.at[o - 1 + 2 * core], buf.at[o], ex_s.at[m, o - 1],
            ex_r.at[m, o - 1], device_id={"ctx": sibling}, device_id_type=MESH)

    own = []
    for m, w in ((0, wk), (1, wv)):
        copy = pltpu.make_async_copy(w, at(m, idx * rows, rows), own_sem.at[m])
        copy.start()
        own.append(copy)

    barrier = pltpu.get_barrier_semaphore()
    greeted = [{"ctx": (idx + o) % n} for o in range(1, REACH + 1)]
    greeted += [{"ctx": (idx + n - o) % n} for o in range(1, REACH + 1)]
    greeted += [{"ctx": 2 * chip_at((pos + o) % chips) + core} for o in (1, chips - 1)]
    greeted += [{"ctx": sibling}]
    if third:
        greeted += [{"parts": 1 - part}]
    for who in greeted:
        pl.semaphore_signal(barrier, inc=1, device_id=who, device_id_type=MESH)
    pl.semaphore_wait(barrier, len(greeted))

    streams = [(m, d) for m in (0, 1) for d in (0, 1)]
    own[0].wait()
    own[1].wait()
    for m, d in streams:
        ring(m, d, 0, 1).start()
    for m, d in streams:
        sib_own(m, d, core).start()
    for o in range(1, REACH + 1):
        @pl.when(idx + o < n)
        def _():
            send_docs(o).start()

        @pl.when(idx < o)
        def _():
            kout[o] = jnp.zeros(kout.shape[1:], kout.dtype)
            vout[o] = jnp.zeros(vout.shape[1:], vout.dtype)
            dout[o] = jnp.full(dout.shape[1:], -1, dout.dtype)
    dout[0] = doc[...]

    @pl.loop(0, tok // 16)
    def _(i):
        r16 = pl.ds(pl.multiple_of(i * 16, 16), 16)
        x = hidden[r16, :].astype(jnp.float32)
        mean = jnp.sum(x * x, -1, keepdims=True) * (1.0 / depth)
        normed[r16, :] = (x * lax.rsqrt(mean + 1e-05)).astype(jnp.bfloat16)

    @pl.loop(1, chips)
    def _(s):
        for m, d in streams:
            ring(m, d, s, s).wait_recv()

            @pl.when(s < chips - 1)
            def _():
                ring(m, d, s, s + 1).start()

            if third:
                cross(m, d, s, part).start()
            sib(m, d, s, core).start()
        if third:
            @pl.when(s > 1)
            def _():
                for m, d in streams:
                    cross(m, d, s - 1, 1 - part).wait_recv()
                    cross_sib(m, d, s - 1, core).start()

    if third:
        for m, d in streams:
            cross(m, d, chips - 1, 1 - part).wait_recv()
            cross_sib(m, d, chips - 1, core).start()

    for m, d in streams:
        sib_own(m, d, 1 - core).wait_recv()

    @pl.loop(1, chips)
    def _(s):
        for m, d in streams:
            sib(m, d, s, 1 - core).wait_recv()
            if third:
                cross_sib(m, d, s, 1 - core).wait_recv()

    step = 1024
    for m in (0, 1):
        for i in range(depth // step):
            part_sum = jnp.dot(normed[:, i * step:(i + 1) * step],
                               w_all[m, i * step:(i + 1) * step, :],
                               preferred_element_type=jnp.float32)
            acc[...] = part_sum if i == 0 else acc[...] + part_sum
        if m == 0:
            for h in range(KV_HEADS):
                cols = slice(h * HEAD_DIM, (h + 1) * HEAD_DIM)
                x = acc[:, cols]
                turned = x * cos2[...] + pltpu.roll(x, HEAD_DIM // 2, 1) * sin2[...]
                kout[0, :, cols] = turned.astype(jnp.bfloat16)
        else:
            vout[0] = acc[...].astype(jnp.bfloat16)
        buf = (kout, vout)[m]
        for o in (2, 4):
            @pl.when(idx + o < n)
            def _():
                send_ahead(m, buf, o).start()

    for m, buf in ((0, kout), (1, vout)):
        for o in (2, 4):
            @pl.when(idx >= o)
            def _():
                send_ahead(m, buf, o).wait_recv()
        for o in (1, 3):
            @pl.when(sibling >= o)
            def _():
                send_beside(m, buf, o).start()
    for m, buf in ((0, kout), (1, vout)):
        for o in (1, 3):
            @pl.when(idx >= o)
            def _():
                send_beside(m, buf, o).wait_recv()

            @pl.when(sibling >= o)
            def _():
                send_beside(m, buf, o).wait_send()
        for o in (2, 4):
            @pl.when(idx + o < n)
            def _():
                send_ahead(m, buf, o).wait_send()
    for o in range(1, REACH + 1):
        @pl.when(idx + o < n)
        def _():
            send_docs(o).wait_send()

        @pl.when(idx >= o)
        def _():
            send_docs(o).wait_recv()

    for m, d in streams:
        ring(m, d, 0, 1).wait_send()
        sib_own(m, d, core).wait_send()

    @pl.loop(1, chips)
    def _(s):
        for m, d in streams:
            @pl.when(s < chips - 1)
            def _():
                ring(m, d, s, s).wait_send()

            sib(m, d, s, core).wait_send()
            if third:
                cross(m, d, s, part).wait_send()
                cross_sib(m, d, s, core).wait_send()


def attend_kernel(q, k, v, key_docs, q_docs, out, bias):
    tok = q.shape[0]
    span = k.shape[0]

    @pl.when(pl.program_id(0) == 0)
    def _():
        same = key_docs[...] == q_docs[...]
        key_at = lax.broadcasted_iota(jnp.int32, (tok, span), 1)
        row = lax.broadcasted_iota(jnp.int32, (tok, span), 0)
        allowed = same & (key_at <= row + jnp.where(key_at >= tok, span, 0))
        bias[...] = jnp.where(allowed, 0.0, -jnp.inf)

    scale = math.log2(math.e) / math.sqrt(HEAD_DIM)
    for g in range(GROUP):
        cols = slice(g * HEAD_DIM, (g + 1) * HEAD_DIM)
        scores = lax.dot_general(q[:, cols], k[...], (((1,), (1,)), ((), ())),
                                 preferred_element_type=jnp.float32) + bias[...]
        top = jnp.max(scores, -1, keepdims=True)
        expo = jnp.exp2((scores - top) * scale)
        total = jnp.sum(expo, -1, keepdims=True)
        probs = (expo * (1.0 / total)).astype(jnp.bfloat16)
        out[:, cols] = jnp.dot(
            probs, v[...], preferred_element_type=jnp.float32).astype(jnp.bfloat16)


def on_device(n, parts, hidden_states, queries, w_key, w_value, doc_ids):
    tok, depth = hidden_states.shape
    kvw = w_key.shape[1]
    half_dim = HEAD_DIM // 2
    inverse_freq = 500000.0 ** (-jnp.arange(half_dim).astype(jnp.float32) * 2.0 / HEAD_DIM)
    positions = lax.axis_index("ctx") * tok + jnp.arange(tok)
    angles = positions.astype(jnp.float32)[:, None] * inverse_freq[None, :]
    cosine, sine = jnp.cos(angles), jnp.sin(angles)
    cos2 = jnp.concatenate([cosine, cosine], -1)
    sin2 = jnp.concatenate([-sine, sine], -1)
    chips = n // 2
    sem = pltpu.SemaphoreType.DMA
    blocks = REACH + 1
    in_vmem = pl.BlockSpec(memory_space=pltpu.VMEM)
    in_any = pl.BlockSpec(memory_space=pl.ANY)
    keys, values, docs = pl.pallas_call(
        functools.partial(project_kernel, n, parts),
        out_shape=(
            jax.ShapeDtypeStruct((blocks, tok, kvw), jnp.bfloat16),
            jax.ShapeDtypeStruct((blocks, tok, kvw), jnp.bfloat16),
            jax.ShapeDtypeStruct((blocks, 1, tok), jnp.int32),
        ),
        in_specs=[in_vmem, in_any, in_any, in_vmem, in_vmem, in_vmem],
        out_specs=(in_vmem, in_vmem, in_vmem),
        scratch_shapes=[
            pltpu.VMEM((2, depth, kvw), jnp.bfloat16),
            pltpu.VMEM((tok, depth), jnp.bfloat16),
            pltpu.VMEM((tok, kvw), jnp.float32),
            sem((2,)),
        ] + [sem((2, 2, chips))] * 8 + [sem((2, REACH))] * 2 + [sem((REACH,))] * 2,
        compiler_params=pltpu.CompilerParams(
            collective_id=0, has_side_effects=True, vmem_limit_bytes=48 * 2**20),
        name="project",
    )(hidden_states, w_key, w_value, cos2, sin2, doc_ids.reshape(1, tok))
    span = blocks * tok
    width = GROUP * HEAD_DIM
    return pl.pallas_call(
        attend_kernel,
        grid=(KV_HEADS,),
        out_shape=jax.ShapeDtypeStruct(queries.shape, jnp.bfloat16),
        in_specs=[
            pl.BlockSpec((tok, width), lambda h: (0, h)),
            pl.BlockSpec((span, HEAD_DIM), lambda h: (0, h)),
            pl.BlockSpec((span, HEAD_DIM), lambda h: (0, h)),
            pl.BlockSpec((1, span), lambda h: (0, 0)),
            pl.BlockSpec((tok, 1), lambda h: (0, 0)),
        ],
        out_specs=pl.BlockSpec((tok, width), lambda h: (0, h)),
        scratch_shapes=[pltpu.VMEM((tok, span), jnp.float32)],
        compiler_params=pltpu.CompilerParams(vmem_limit_bytes=48 * 2**20),
        name="attend",
    )(queries, keys.reshape(span, kvw), values.reshape(span, kvw),
      docs.reshape(1, span), doc_ids.reshape(tok, 1))


def solution(mesh):
    in_specs = (
        P(("parts", "ctx"), None),
        P(("parts", "ctx"), None),
        P("ctx", None),
        P("ctx", None),
        P(("parts", "ctx")),
    )
    out_specs = P(("parts", "ctx"), None)
    return jax.shard_map(
        functools.partial(on_device, mesh.shape["ctx"], mesh.shape["parts"]),
        mesh=mesh, in_specs=in_specs, out_specs=out_specs, check_vma=False
    )
```

```python
import functools
import math

import jax
import jax.numpy as jnp
from jax import lax
from jax.experimental import pallas as pl
from jax.experimental.pallas import tpu as pltpu
from jax.sharding import PartitionSpec as P

HEAD_DIM = 128
HEADS = 32
KV_HEADS = 4
REACH = 4
GROUP = HEADS // KV_HEADS
MESH = pl.DeviceIdType.MESH


def fused_kernel(n, parts, hidden, queries, wk, wv, cos2, sin2, doc, out,
                 w_all, normed, q_all, probs, bias, acc, kbuf, vbuf, dbuf,
                 own_sem, ring_s, ring_r, sib_s, sib_r, x_s, x_r,
                 xs_s, xs_r, ex_s, ex_r, doc_s, doc_r):
    chips = n // 2
    rows = wk.shape[0]
    half = rows // 2
    third = (half // 48) * 16 if parts == 2 else 0
    length = half - third
    first = (length // 32) * 16
    subs = ((0, first), (first, length - first))
    tok, depth = hidden.shape
    blocks = REACH + 1
    span = blocks * tok

    idx = lax.axis_index("ctx")
    part = lax.axis_index("parts")
    core = idx % 2
    chip_no = idx // 2
    col = chip_no % 2
    lane = chip_no // 2
    pos = col * (chips - 1 - lane) + (1 - col) * lane
    sibling = idx + 1 - 2 * core

    def chip_at(place):
        upper = place // (chips // 2)
        return (1 - upper) * 2 * place + upper * (2 * (chips - 1 - place) + 1)

    def base(d, s, which_core):
        owner = (pos + chips - s) % chips if d == 0 else (pos + s) % chips
        return (2 * chip_at(owner) + which_core) * rows + d * half

    def at(m, start, count):
        return w_all.at[m, pl.ds(pl.multiple_of(start, 16), count), :]

    def ring(m, d, u, s, recv_s):
        target = (pos + 1) % chips if d == 0 else (pos + chips - 1) % chips
        piece = at(m, base(d, s, core) + part * third + subs[u][0], subs[u][1])
        return pltpu.make_async_remote_copy(
            piece, piece, ring_s.at[m, d, u, s], ring_r.at[m, d, u, recv_s],
            device_id={"ctx": 2 * chip_at(target) + core}, device_id_type=MESH)

    def sib_own(m, d, which_core):
        piece = at(m, base(d, 0, which_core), half)
        return pltpu.make_async_remote_copy(
            piece, piece, sib_s.at[m, d, 0], sib_r.at[m, d, 0],
            device_id={"ctx": sibling}, device_id_type=MESH)

    def sib(m, d, s, which_core):
        piece = at(m, base(d, s, which_core) + part * third, length)
        return pltpu.make_async_remote_copy(
            piece, piece, sib_s.at[m, d, s], sib_r.at[m, d, s],
            device_id={"ctx": sibling}, device_id_type=MESH)

    def cross(m, d, s, of_part):
        piece = at(m, base(d, s, core) + of_part * (half - third), third)
        return pltpu.make_async_remote_copy(
            piece, piece, x_s.at[m, d, s], x_r.at[m, d, s],
            device_id={"parts": 1 - part}, device_id_type=MESH)

    def cross_sib(m, d, s, which_core):
        piece = at(m, base(d, s, which_core) + (1 - part) * (half - third), third)
        return pltpu.make_async_remote_copy(
            piece, piece, xs_s.at[m, d, s], xs_r.at[m, d, s],
            device_id={"ctx": sibling}, device_id_type=MESH)

    def send_docs(o):
        return pltpu.make_async_remote_copy(
            doc, dbuf.at[o], doc_s.at[o - 1], doc_r.at[o - 1],
            device_id={"ctx": (idx + o) % n}, device_id_type=MESH)

    kvw = wk.shape[1]
    groups = ((kbuf, slice(0, kvw)), (vbuf, slice(0, kvw // 2)), (vbuf, slice(kvw // 2, kvw)))

    def send_ahead(e, o):
        buf, cols = groups[e]
        return pltpu.make_async_remote_copy(
            buf.at[0, :, cols], buf.at[o, :, cols], ex_s.at[e, o - 1], ex_r.at[e, o - 1],
            device_id={"ctx": (idx + o) % n}, device_id_type=MESH)

    def send_beside(e, o):
        buf, cols = groups[e]
        return pltpu.make_async_remote_copy(
            buf.at[o - 1 + 2 * core, :, cols], buf.at[o, :, cols], ex_s.at[e, o - 1],
            ex_r.at[e, o - 1], device_id={"ctx": sibling}, device_id_type=MESH)

    def pass_on(e):
        for o in (2, 4):
            @pl.when(idx + o < n)
            def _():
                send_ahead(e, o).start()

    def pass_beside(e):
        for o in (2, 4):
            @pl.when(idx >= o)
            def _():
                send_ahead(e, o).wait_recv()
        for o in (1, 3):
            @pl.when(sibling >= o)
            def _():
                send_beside(e, o).start()

    def passed(e):
        for o in (1, 3):
            @pl.when(idx >= o)
            def _():
                send_beside(e, o).wait_recv()

    own = [pltpu.make_async_copy(w, at(m, idx * rows, rows), own_sem.at[m])
           for m, w in ((0, wk), (1, wv))]
    own += [pltpu.make_async_copy(hidden, normed, own_sem.at[2]),
            pltpu.make_async_copy(queries, q_all, own_sem.at[3])]
    for copy in own:
        copy.start()

    barrier = pltpu.get_barrier_semaphore()
    greeted = [{"ctx": (idx + o) % n} for o in range(1, REACH + 1)]
    greeted += [{"ctx": (idx + n - o) % n} for o in range(1, REACH + 1)]
    greeted += [{"ctx": 2 * chip_at((pos + o) % chips) + core} for o in (1, chips - 1)]
    greeted += [{"ctx": sibling}]
    if third:
        greeted += [{"parts": 1 - part}]
    for who in greeted:
        pl.semaphore_signal(barrier, inc=1, device_id=who, device_id_type=MESH)
    pl.semaphore_wait(barrier, len(greeted))

    ways = (0, 1)

    def begin(m):
        for u in (0, 1):
            for d in ways:
                ring(m, d, u, 0, 1).start()
        for d in ways:
            sib_own(m, d, core).start()

    def turn(m, s):
        for u in (0, 1):
            for d in ways:
                ring(m, d, u, s, s).wait_recv()

                @pl.when(s < chips - 1)
                def _():
                    ring(m, d, u, s, s + 1).start()
        for d in ways:
            if third:
                cross(m, d, s, part).start()
            sib(m, d, s, core).start()
        if third:
            @pl.when(s > 1)
            def _():
                for d in ways:
                    cross(m, d, s - 1, 1 - part).wait_recv()
                    cross_sib(m, d, s - 1, core).start()

    def last_cross(m):
        if third:
            for d in ways:
                cross(m, d, chips - 1, 1 - part).wait_recv()
                cross_sib(m, d, chips - 1, core).start()

    def gathered(m):
        for d in ways:
            sib_own(m, d, 1 - core).wait_recv()

        @pl.loop(1, chips)
        def _(s):
            for d in ways:
                sib(m, d, s, 1 - core).wait_recv()
                if third:
                    cross_sib(m, d, s, 1 - core).wait_recv()

    def project(m, cols):
        step = 1024
        for i in range(depth // step):
            part_sum = jnp.dot(normed[:, i * step:(i + 1) * step],
                               w_all[m, i * step:(i + 1) * step, cols],
                               preferred_element_type=jnp.float32)
            acc[:, cols] = part_sum if i == 0 else acc[:, cols] + part_sum

    own[0].wait()
    begin(0)
    own[1].wait()
    for o in range(1, blocks):
        @pl.when(idx + o < n)
        def _():
            send_docs(o).start()

        @pl.when(idx < o)
        def _():
            kbuf[o] = jnp.zeros(kbuf.shape[1:], kbuf.dtype)
            vbuf[o] = jnp.zeros(vbuf.shape[1:], vbuf.dtype)
            dbuf[o] = jnp.full(dbuf.shape[1:], -1, dbuf.dtype)
    dbuf[0] = doc[...]
    own[2].wait()

    @pl.loop(0, tok // 16)
    def _(i):
        r16 = pl.ds(pl.multiple_of(i * 16, 16), 16)
        x = normed[r16, :].astype(jnp.float32)
        mean = jnp.sum(x * x, -1, keepdims=True) * (1.0 / depth)
        normed[r16, :] = (x * lax.rsqrt(mean + 1e-05)).astype(jnp.bfloat16)

    own[3].wait()

    @pl.loop(1, chips)
    def _(s):
        turn(0, s)

        @pl.when(s == chips - 2)
        def _():
            begin(1)

    for o in range(1, blocks):
        @pl.when(idx >= o)
        def _():
            send_docs(o).wait_recv()
    q_docs = jnp.transpose(jnp.broadcast_to(doc[...], (tok, tok)))
    for b in range(blocks):
        allowed = dbuf[b] == q_docs
        if b == 0:
            allowed &= (lax.broadcasted_iota(jnp.int32, (tok, tok), 1)
                        <= lax.broadcasted_iota(jnp.int32, (tok, tok), 0))
        bias[:, b * tok:(b + 1) * tok] = jnp.where(allowed, 0.0, -jnp.inf)

    last_cross(0)
    gathered(0)
    turn(1, 1)
    project(0, slice(0, kvw))
    for h in range(KV_HEADS):
        cols = slice(h * HEAD_DIM, (h + 1) * HEAD_DIM)
        x = acc[:, cols]
        turned = x * cos2[...] + pltpu.roll(x, HEAD_DIM // 2, 1) * sin2[...]
        kbuf[0, :, cols] = turned.astype(jnp.bfloat16)
    pass_on(0)
    turn(1, 2)
    pass_beside(0)
    turn(1, 3)
    passed(0)

    @pl.loop(4, chips - 4)
    def _(s):
        turn(1, s)

    scale = math.log2(math.e) / math.sqrt(HEAD_DIM)
    per_step = 2

    @pl.loop(0, HEADS // per_step)
    def _(i):
        @pl.when((i % 3 == 0) & (i < 12))
        def _():
            turn(1, chips - 4 + i // 3)

        @pl.when(i == 12)
        def _():
            last_cross(1)

        for g in range(per_step):
            h = i * per_step + g
            q = q_all[:, pl.ds(pl.multiple_of(h * HEAD_DIM, HEAD_DIM), HEAD_DIM)]
            k_cols = pl.ds(pl.multiple_of((h // GROUP) * HEAD_DIM, HEAD_DIM), HEAD_DIM)
            k = kbuf[:, :, k_cols].reshape(span, HEAD_DIM)
            scores = lax.dot_general(q, k, (((1,), (1,)), ((), ())),
                                     preferred_element_type=jnp.float32) + bias[...]
            top = jnp.max(scores, -1, keepdims=True)
            expo = jnp.exp2((scores - top) * scale)
            total = jnp.sum(expo, -1, keepdims=True)
            probs[h] = (expo * (1.0 / total)).astype(jnp.bfloat16)

    gathered(1)
    for e in (1, 2):
        cols = groups[e][1]
        project(1, cols)
        vbuf[0, :, cols] = acc[:, cols].astype(jnp.bfloat16)
        pass_on(e)
    pass_beside(1)
    pass_beside(2)
    for e in (1, 2):
        passed(e)

        @pl.loop((e - 1) * HEADS // 2 // per_step, e * HEADS // 2 // per_step)
        def _(i):
            for g in range(per_step):
                h = i * per_step + g
                v_cols = pl.ds(pl.multiple_of((h // GROUP) * HEAD_DIM, HEAD_DIM), HEAD_DIM)
                v = vbuf[:, :, v_cols].reshape(span, HEAD_DIM)
                out[:, pl.ds(pl.multiple_of(h * HEAD_DIM, HEAD_DIM), HEAD_DIM)] = jnp.dot(
                    probs[h], v, preferred_element_type=jnp.float32).astype(jnp.bfloat16)

    for e in range(3):
        for o in (1, 3):
            @pl.when(sibling >= o)
            def _():
                send_beside(e, o).wait_send()
        for o in (2, 4):
            @pl.when(idx + o < n)
            def _():
                send_ahead(e, o).wait_send()
    for o in range(1, blocks):
        @pl.when(idx + o < n)
        def _():
            send_docs(o).wait_send()

    for m in (0, 1):
        for d in ways:
            for u in (0, 1):
                ring(m, d, u, 0, 1).wait_send()
            sib_own(m, d, core).wait_send()

    @pl.loop(1, chips)
    def _(s):
        for m in (0, 1):
            for d in ways:
                @pl.when(s < chips - 1)
                def _():
                    for u in (0, 1):
                        ring(m, d, u, s, s).wait_send()

                sib(m, d, s, core).wait_send()
                if third:
                    cross(m, d, s, part).wait_send()
                    cross_sib(m, d, s, core).wait_send()


def on_device(n, parts, hidden_states, queries, w_key, w_value, doc_ids):
    tok, depth = hidden_states.shape
    kvw = w_key.shape[1]
    half_dim = HEAD_DIM // 2
    inverse_freq = 500000.0 ** (-jnp.arange(half_dim).astype(jnp.float32) * 2.0 / HEAD_DIM)
    positions = lax.axis_index("ctx") * tok + jnp.arange(tok)
    angles = positions.astype(jnp.float32)[:, None] * inverse_freq[None, :]
    cosine, sine = jnp.cos(angles), jnp.sin(angles)
    cos2 = jnp.concatenate([cosine, cosine], -1)
    sin2 = jnp.concatenate([-sine, sine], -1)
    chips = n // 2
    sem = pltpu.SemaphoreType.DMA
    blocks = REACH + 1
    in_vmem = pl.BlockSpec(memory_space=pltpu.VMEM)
    in_any = pl.BlockSpec(memory_space=pl.ANY)
    return pl.pallas_call(
        functools.partial(fused_kernel, n, parts),
        out_shape=jax.ShapeDtypeStruct(queries.shape, jnp.bfloat16),
        in_specs=[in_any, in_any, in_any, in_any, in_vmem, in_vmem, in_vmem],
        out_specs=in_vmem,
        scratch_shapes=[
            pltpu.VMEM((2, depth, kvw), jnp.bfloat16),
            pltpu.VMEM((tok, depth), jnp.bfloat16),
            pltpu.VMEM(queries.shape, jnp.bfloat16),
            pltpu.VMEM((HEADS, tok, blocks * tok), jnp.bfloat16),
            pltpu.VMEM((tok, blocks * tok), jnp.float32),
            pltpu.VMEM((tok, kvw), jnp.float32),
            pltpu.VMEM((blocks, tok, kvw), jnp.bfloat16),
            pltpu.VMEM((blocks, tok, kvw), jnp.bfloat16),
            pltpu.VMEM((blocks, 1, tok), jnp.int32),
            sem((4,)),
        ] + [sem((2, 2, 2, chips))] * 2 + [sem((2, 2, chips))] * 6
        + [sem((3, REACH))] * 2 + [sem((REACH,))] * 2,
        compiler_params=pltpu.CompilerParams(
            collective_id=0, has_side_effects=True, vmem_limit_bytes=60 * 2**20),
        name="project_attend",
    )(hidden_states, queries, w_key, w_value, cos2, sin2, doc_ids.reshape(1, tok))


def solution(mesh):
    in_specs = (
        P(("parts", "ctx"), None),
        P(("parts", "ctx"), None),
        P("ctx", None),
        P("ctx", None),
        P(("parts", "ctx")),
    )
    out_specs = P(("parts", "ctx"), None)
    return jax.shard_map(
        functools.partial(on_device, mesh.shape["ctx"], mesh.shape["parts"]),
        mesh=mesh, in_specs=in_specs, out_specs=out_specs, check_vma=False
    )
```

```python
import functools
import math

import jax
import jax.numpy as jnp
from jax import lax
from jax.experimental import pallas as pl
from jax.experimental.pallas import tpu as pltpu
from jax.sharding import PartitionSpec as P

HEAD_DIM = 128
HEADS = 32
KV_HEADS = 4
REACH = 4
GROUP = HEADS // KV_HEADS
MESH = pl.DeviceIdType.MESH


def fused_kernel(n, parts, hidden, queries, wk, wv, cos2, sin2, doc, out,
                 w_all, normed, q_all, probs, bias, acc, kbuf, vbuf, dbuf,
                 own_sem, ring_s, ring_r, sib_s, sib_r, x_s, x_r,
                 xs_s, xs_r, ex_s, ex_r, doc_s, doc_r):
    chips = n // 2
    rows = wk.shape[0]
    half = rows // 2
    third = (half // 48) * 16 if parts == 2 else 0
    length = half - third
    first = (length // 32) * 16
    subs = ((0, first), (first, length - first))
    piecewise = half % 128 == 0
    tok, depth = hidden.shape
    blocks = REACH + 1
    span = blocks * tok

    idx = lax.axis_index("ctx")
    part = lax.axis_index("parts")
    core = idx % 2
    chip_no = idx // 2
    col = chip_no % 2
    lane = chip_no // 2
    pos = col * (chips - 1 - lane) + (1 - col) * lane
    sibling = idx + 1 - 2 * core

    def chip_at(place):
        upper = place // (chips // 2)
        return (1 - upper) * 2 * place + upper * (2 * (chips - 1 - place) + 1)

    def base(d, s, which_core):
        owner = (pos + chips - s) % chips if d == 0 else (pos + s) % chips
        return (2 * chip_at(owner) + which_core) * rows + d * half

    def at(m, start, count):
        return w_all.at[m, pl.ds(pl.multiple_of(start, 16), count), :]

    def ring(m, d, u, s, recv_s):
        target = (pos + 1) % chips if d == 0 else (pos + chips - 1) % chips
        piece = at(m, base(d, s, core) + part * third + subs[u][0], subs[u][1])
        return pltpu.make_async_remote_copy(
            piece, piece, ring_s.at[m, d, u, s], ring_r.at[m, d, u, recv_s],
            device_id={"ctx": 2 * chip_at(target) + core}, device_id_type=MESH)

    def sib_own(m, d, which_core):
        piece = at(m, base(d, 0, which_core), half)
        return pltpu.make_async_remote_copy(
            piece, piece, sib_s.at[m, d, 0], sib_r.at[m, d, 0],
            device_id={"ctx": sibling}, device_id_type=MESH)

    def sib(m, d, s, which_core):
        piece = at(m, base(d, s, which_core) + part * third, length)
        return pltpu.make_async_remote_copy(
            piece, piece, sib_s.at[m, d, s], sib_r.at[m, d, s],
            device_id={"ctx": sibling}, device_id_type=MESH)

    def cross(m, d, s, of_part):
        piece = at(m, base(d, s, core) + of_part * (half - third), third)
        return pltpu.make_async_remote_copy(
            piece, piece, x_s.at[m, d, s], x_r.at[m, d, s],
            device_id={"parts": 1 - part}, device_id_type=MESH)

    def cross_sib(m, d, s, which_core):
        piece = at(m, base(d, s, which_core) + (1 - part) * (half - third), third)
        return pltpu.make_async_remote_copy(
            piece, piece, xs_s.at[m, d, s], xs_r.at[m, d, s],
            device_id={"ctx": sibling}, device_id_type=MESH)

    def send_docs(o):
        return pltpu.make_async_remote_copy(
            doc, dbuf.at[o], doc_s.at[o - 1], doc_r.at[o - 1],
            device_id={"ctx": (idx + o) % n}, device_id_type=MESH)

    kvw = wk.shape[1]
    groups = ((kbuf, slice(0, kvw)), (vbuf, slice(0, kvw // 2)), (vbuf, slice(kvw // 2, kvw)))

    def send_ahead(e, o):
        buf, cols = groups[e]
        return pltpu.make_async_remote_copy(
            buf.at[0, :, cols], buf.at[o, :, cols], ex_s.at[e, o - 1], ex_r.at[e, o - 1],
            device_id={"ctx": (idx + o) % n}, device_id_type=MESH)

    def send_beside(e, o):
        buf, cols = groups[e]
        return pltpu.make_async_remote_copy(
            buf.at[o - 1 + 2 * core, :, cols], buf.at[o, :, cols], ex_s.at[e, o - 1],
            ex_r.at[e, o - 1], device_id={"ctx": sibling}, device_id_type=MESH)

    def pass_on(e):
        for o in (2, 4):
            @pl.when(idx + o < n)
            def _():
                send_ahead(e, o).start()

    def pass_beside(e):
        for o in (2, 4):
            @pl.when(idx >= o)
            def _():
                send_ahead(e, o).wait_recv()
        for o in (1, 3):
            @pl.when(sibling >= o)
            def _():
                send_beside(e, o).start()

    def passed(e):
        for o in (1, 3):
            @pl.when(idx >= o)
            def _():
                send_beside(e, o).wait_recv()

    own = [pltpu.make_async_copy(w, at(m, idx * rows, rows), own_sem.at[m])
           for m, w in ((0, wk), (1, wv))]
    own += [pltpu.make_async_copy(hidden, normed, own_sem.at[2]),
            pltpu.make_async_copy(queries, q_all, own_sem.at[3])]
    for copy in own:
        copy.start()

    barrier = pltpu.get_barrier_semaphore()
    greeted = [{"ctx": (idx + o) % n} for o in range(1, REACH + 1)]
    greeted += [{"ctx": (idx + n - o) % n} for o in range(1, REACH + 1)]
    greeted += [{"ctx": 2 * chip_at((pos + o) % chips) + core} for o in (1, chips - 1)]
    greeted += [{"ctx": sibling}]
    if third:
        greeted += [{"parts": 1 - part}]
    for who in greeted:
        pl.semaphore_signal(barrier, inc=1, device_id=who, device_id_type=MESH)
    pl.semaphore_wait(barrier, len(greeted))

    ways = (0, 1)

    def begin(m):
        for u in (0, 1):
            for d in ways:
                ring(m, d, u, 0, 1).start()
        for d in ways:
            sib_own(m, d, core).start()

    def turn(m, s):
        for u in (0, 1):
            for d in ways:
                ring(m, d, u, s, s).wait_recv()

                @pl.when(s < chips - 1)
                def _():
                    ring(m, d, u, s, s + 1).start()
        for d in ways:
            if third:
                cross(m, d, s, part).start()
            sib(m, d, s, core).start()
        if third:
            @pl.when(s > 1)
            def _():
                for d in ways:
                    cross(m, d, s - 1, 1 - part).wait_recv()
                    cross_sib(m, d, s - 1, core).start()
        if piecewise:
            @pl.when(s > 1)
            def _():
                absorb(m, s - 2)

    def absorb(m, s):
        @pl.when(s == 0)
        def _():
            for d in ways:
                sib_own(m, d, 1 - core).wait_recv()
            acc[...] = jnp.zeros_like(acc)

        @pl.when(s > 0)
        def _():
            for d in ways:
                sib(m, d, s, 1 - core).wait_recv()
                if third:
                    cross_sib(m, d, s, 1 - core).wait_recv()

        total = acc[...]
        for d in ways:
            for c in (0, 1):
                start = base(d, s, c)
                total += jnp.dot(
                    normed[:, pl.ds(pl.multiple_of(start, 128), half)], at(m, start, half)[...],
                    preferred_element_type=jnp.float32)
        acc[...] = total

    def last_cross(m):
        if third:
            for d in ways:
                cross(m, d, chips - 1, 1 - part).wait_recv()
                cross_sib(m, d, chips - 1, core).start()

    def gathered(m):
        if piecewise:
            absorb(m, chips - 2)
            absorb(m, chips - 1)
            return
        for d in ways:
            sib_own(m, d, 1 - core).wait_recv()

        @pl.loop(1, chips)
        def _(s):
            for d in ways:
                sib(m, d, s, 1 - core).wait_recv()
                if third:
                    cross_sib(m, d, s, 1 - core).wait_recv()

    def project(m, cols):
        if piecewise:
            return
        step = 1024
        for i in range(depth // step):
            part_sum = jnp.dot(normed[:, i * step:(i + 1) * step],
                               w_all[m, i * step:(i + 1) * step, cols],
                               preferred_element_type=jnp.float32)
            acc[:, cols] = part_sum if i == 0 else acc[:, cols] + part_sum

    own[0].wait()
    begin(0)
    own[1].wait()
    for o in range(1, blocks):
        @pl.when(idx + o < n)
        def _():
            send_docs(o).start()

        @pl.when(idx < o)
        def _():
            kbuf[o] = jnp.zeros(kbuf.shape[1:], kbuf.dtype)
            vbuf[o] = jnp.zeros(vbuf.shape[1:], vbuf.dtype)
            dbuf[o] = jnp.full(dbuf.shape[1:], -1, dbuf.dtype)
    dbuf[0] = doc[...]
    own[2].wait()

    @pl.loop(0, tok // 16)
    def _(i):
        r16 = pl.ds(pl.multiple_of(i * 16, 16), 16)
        x = normed[r16, :].astype(jnp.float32)
        mean = jnp.sum(x * x, -1, keepdims=True) * (1.0 / depth)
        normed[r16, :] = (x * lax.rsqrt(mean + 1e-05)).astype(jnp.bfloat16)

    own[3].wait()

    @pl.loop(1, chips)
    def _(s):
        turn(0, s)

        @pl.when(s == chips - 2)
        def _():
            begin(1)

    for o in range(1, blocks):
        @pl.when(idx >= o)
        def _():
            send_docs(o).wait_recv()
    q_docs = jnp.transpose(jnp.broadcast_to(doc[...], (tok, tok)))
    for b in range(blocks):
        allowed = dbuf[b] == q_docs
        if b == 0:
            allowed &= (lax.broadcasted_iota(jnp.int32, (tok, tok), 1)
                        <= lax.broadcasted_iota(jnp.int32, (tok, tok), 0))
        bias[:, b * tok:(b + 1) * tok] = jnp.where(allowed, 0.0, -jnp.inf)

    last_cross(0)
    gathered(0)
    turn(1, 1)
    project(0, slice(0, kvw))
    for h in range(KV_HEADS):
        cols = slice(h * HEAD_DIM, (h + 1) * HEAD_DIM)
        x = acc[:, cols]
        turned = x * cos2[...] + pltpu.roll(x, HEAD_DIM // 2, 1) * sin2[...]
        kbuf[0, :, cols] = turned.astype(jnp.bfloat16)
    pass_on(0)
    turn(1, 2)
    pass_beside(0)
    turn(1, 3)
    passed(0)

    @pl.loop(4, chips - 4)
    def _(s):
        turn(1, s)

    scale = math.log2(math.e) / math.sqrt(HEAD_DIM)
    per_step = 2

    @pl.loop(0, HEADS // per_step)
    def _(i):
        @pl.when((i % 3 == 0) & (i < 12))
        def _():
            turn(1, chips - 4 + i // 3)

        @pl.when(i == 12)
        def _():
            last_cross(1)

        for g in range(per_step):
            h = i * per_step + g
            q = q_all[:, pl.ds(pl.multiple_of(h * HEAD_DIM, HEAD_DIM), HEAD_DIM)]
            k_cols = pl.ds(pl.multiple_of((h // GROUP) * HEAD_DIM, HEAD_DIM), HEAD_DIM)
            k = kbuf[:, :, k_cols].reshape(span, HEAD_DIM)
            scores = lax.dot_general(q, k, (((1,), (1,)), ((), ())),
                                     preferred_element_type=jnp.float32) + bias[...]
            top = jnp.max(scores, -1, keepdims=True)
            expo = jnp.exp2((scores - top) * scale)
            total = jnp.sum(expo, -1, keepdims=True)
            probs[h] = (expo * (1.0 / total)).astype(jnp.bfloat16)

    gathered(1)
    for e in (1, 2):
        cols = groups[e][1]
        project(1, cols)
        vbuf[0, :, cols] = acc[:, cols].astype(jnp.bfloat16)
        pass_on(e)
    pass_beside(1)
    pass_beside(2)
    for e in (1, 2):
        passed(e)

        @pl.loop((e - 1) * HEADS // 2 // per_step, e * HEADS // 2 // per_step)
        def _(i):
            for g in range(per_step):
                h = i * per_step + g
                v_cols = pl.ds(pl.multiple_of((h // GROUP) * HEAD_DIM, HEAD_DIM), HEAD_DIM)
                v = vbuf[:, :, v_cols].reshape(span, HEAD_DIM)
                out[:, pl.ds(pl.multiple_of(h * HEAD_DIM, HEAD_DIM), HEAD_DIM)] = jnp.dot(
                    probs[h], v, preferred_element_type=jnp.float32).astype(jnp.bfloat16)

    for e in range(3):
        for o in (1, 3):
            @pl.when(sibling >= o)
            def _():
                send_beside(e, o).wait_send()
        for o in (2, 4):
            @pl.when(idx + o < n)
            def _():
                send_ahead(e, o).wait_send()
    for o in range(1, blocks):
        @pl.when(idx + o < n)
        def _():
            send_docs(o).wait_send()

    for m in (0, 1):
        for d in ways:
            for u in (0, 1):
                ring(m, d, u, 0, 1).wait_send()
            sib_own(m, d, core).wait_send()

    @pl.loop(1, chips)
    def _(s):
        for m in (0, 1):
            for d in ways:
                @pl.when(s < chips - 1)
                def _():
                    for u in (0, 1):
                        ring(m, d, u, s, s).wait_send()

                sib(m, d, s, core).wait_send()
                if third:
                    cross(m, d, s, part).wait_send()
                    cross_sib(m, d, s, core).wait_send()


def on_device(n, parts, hidden_states, queries, w_key, w_value, doc_ids):
    tok, depth = hidden_states.shape
    kvw = w_key.shape[1]
    half_dim = HEAD_DIM // 2
    place = jnp.arange(HEAD_DIM)
    inverse_freq = 500000.0 ** (-(place % half_dim).astype(jnp.float32) * 2.0 / HEAD_DIM)
    positions = lax.axis_index("ctx") * tok + jnp.arange(tok)
    angles = positions.astype(jnp.float32)[:, None] * inverse_freq[None, :]
    cos2 = jnp.cos(angles)
    sin2 = jnp.sin(angles) * jnp.where(place < half_dim, -1.0, 1.0)[None, :]
    chips = n // 2
    sem = pltpu.SemaphoreType.DMA
    blocks = REACH + 1
    in_vmem = pl.BlockSpec(memory_space=pltpu.VMEM)
    in_any = pl.BlockSpec(memory_space=pl.ANY)
    return pl.pallas_call(
        functools.partial(fused_kernel, n, parts),
        out_shape=jax.ShapeDtypeStruct(queries.shape, jnp.bfloat16),
        in_specs=[in_any, in_any, in_any, in_any, in_vmem, in_vmem, in_vmem],
        out_specs=in_vmem,
        scratch_shapes=[
            pltpu.VMEM((2, depth, kvw), jnp.bfloat16),
            pltpu.VMEM((tok, depth), jnp.bfloat16),
            pltpu.VMEM(queries.shape, jnp.bfloat16),
            pltpu.VMEM((HEADS, tok, blocks * tok), jnp.bfloat16),
            pltpu.VMEM((tok, blocks * tok), jnp.float32),
            pltpu.VMEM((tok, kvw), jnp.float32),
            pltpu.VMEM((blocks, tok, kvw), jnp.bfloat16),
            pltpu.VMEM((blocks, tok, kvw), jnp.bfloat16),
            pltpu.VMEM((blocks, 1, tok), jnp.int32),
            sem((4,)),
        ] + [sem((2, 2, 2, chips))] * 2 + [sem((2, 2, chips))] * 6
        + [sem((3, REACH))] * 2 + [sem((REACH,))] * 2,
        compiler_params=pltpu.CompilerParams(
            collective_id=0, has_side_effects=True, vmem_limit_bytes=60 * 2**20),
        name="project_attend",
    )(hidden_states, queries, w_key, w_value, cos2, sin2, doc_ids.reshape(1, tok))


def solution(mesh):
    in_specs = (
        P(("parts", "ctx"), None),
        P(("parts", "ctx"), None),
        P("ctx", None),
        P("ctx", None),
        P(("parts", "ctx")),
    )
    out_specs = P(("parts", "ctx"), None)
    return jax.shard_map(
        functools.partial(on_device, mesh.shape["ctx"], mesh.shape["parts"]),
        mesh=mesh, in_specs=in_specs, out_specs=out_specs, check_vma=False
    )
```

```python
import functools
import math

import jax
import jax.numpy as jnp
from jax import lax
from jax.experimental import pallas as pl
from jax.experimental.pallas import tpu as pltpu
from jax.sharding import PartitionSpec as P

HEAD_DIM = 128
HEADS = 32
KV_HEADS = 4
REACH = 4
GROUP = HEADS // KV_HEADS
MESH = pl.DeviceIdType.MESH


def fused_kernel(n, parts, hidden, queries, wk, wv, cos2, sin2, doc, out,
                 w_all, normed, q_all, probs, bias, acc, kbuf, vbuf, dbuf,
                 own_sem, ring_s, ring_r, sib_s, sib_r, x_s, x_r,
                 xs_s, xs_r, ex_s, ex_r, doc_s, doc_r):
    chips = n // 2
    rows = wk.shape[0]
    half = rows // 2
    third = (half // 48) * 16 if parts == 2 else 0
    length = half - third
    first = (length // 32) * 16
    subs = ((0, first), (first, length - first))
    piecewise = half % 128 == 0
    tok, depth = hidden.shape
    blocks = REACH + 1
    span = blocks * tok

    idx = lax.axis_index("ctx")
    part = lax.axis_index("parts")
    core = idx % 2
    chip_no = idx // 2
    col = chip_no % 2
    lane = chip_no // 2
    pos = col * (chips - 1 - lane) + (1 - col) * lane
    sibling = idx + 1 - 2 * core

    def chip_at(place):
        upper = place // (chips // 2)
        return (1 - upper) * 2 * place + upper * (2 * (chips - 1 - place) + 1)

    def base(d, s, which_core):
        owner = (pos + chips - s) % chips if d == 0 else (pos + s) % chips
        return (2 * chip_at(owner) + which_core) * rows + d * half

    def at(m, start, count):
        return w_all.at[m, pl.ds(pl.multiple_of(start, 16), count), :]

    def ring(m, d, u, s, recv_s):
        target = (pos + 1) % chips if d == 0 else (pos + chips - 1) % chips
        piece = at(m, base(d, s, core) + part * third + subs[u][0], subs[u][1])
        return pltpu.make_async_remote_copy(
            piece, piece, ring_s.at[m, d, u, s], ring_r.at[m, d, u, recv_s],
            device_id={"ctx": 2 * chip_at(target) + core}, device_id_type=MESH)

    def sib_own(m, d, which_core):
        piece = at(m, base(d, 0, which_core), half)
        return pltpu.make_async_remote_copy(
            piece, piece, sib_s.at[m, d, 0], sib_r.at[m, d, 0],
            device_id={"ctx": sibling}, device_id_type=MESH)

    def sib(m, d, s, which_core):
        piece = at(m, base(d, s, which_core) + part * third, length)
        return pltpu.make_async_remote_copy(
            piece, piece, sib_s.at[m, d, s], sib_r.at[m, d, s],
            device_id={"ctx": sibling}, device_id_type=MESH)

    def cross(m, d, s, of_part):
        piece = at(m, base(d, s, core) + of_part * (half - third), third)
        return pltpu.make_async_remote_copy(
            piece, piece, x_s.at[m, d, s], x_r.at[m, d, s],
            device_id={"parts": 1 - part}, device_id_type=MESH)

    def cross_sib(m, d, s, which_core):
        piece = at(m, base(d, s, which_core) + (1 - part) * (half - third), third)
        return pltpu.make_async_remote_copy(
            piece, piece, xs_s.at[m, d, s], xs_r.at[m, d, s],
            device_id={"ctx": sibling}, device_id_type=MESH)

    def send_docs(o):
        return pltpu.make_async_remote_copy(
            doc, dbuf.at[o], doc_s.at[o - 1], doc_r.at[o - 1],
            device_id={"ctx": (idx + o) % n}, device_id_type=MESH)

    kvw = wk.shape[1]
    groups = ((kbuf, slice(0, kvw)), (vbuf, slice(0, kvw // 2)), (vbuf, slice(kvw // 2, kvw)))

    def send_ahead(e, o):
        buf, cols = groups[e]
        return pltpu.make_async_remote_copy(
            buf.at[0, :, cols], buf.at[o, :, cols], ex_s.at[e, o - 1], ex_r.at[e, o - 1],
            device_id={"ctx": (idx + o) % n}, device_id_type=MESH)

    def send_beside(e, o):
        buf, cols = groups[e]
        return pltpu.make_async_remote_copy(
            buf.at[o - 1 + 2 * core, :, cols], buf.at[o, :, cols], ex_s.at[e, o - 1],
            ex_r.at[e, o - 1], device_id={"ctx": sibling}, device_id_type=MESH)

    def pass_on(e):
        for o in (2, 4):
            @pl.when(idx + o < n)
            def _():
                send_ahead(e, o).start()

    def pass_beside(e):
        for o in (2, 4):
            @pl.when(idx >= o)
            def _():
                send_ahead(e, o).wait_recv()
        for o in (1, 3):
            @pl.when(sibling >= o)
            def _():
                send_beside(e, o).start()

    def passed(e):
        for o in (1, 3):
            @pl.when(idx >= o)
            def _():
                send_beside(e, o).wait_recv()

    own = [pltpu.make_async_copy(w, at(m, idx * rows, rows), own_sem.at[m])
           for m, w in ((0, wk), (1, wv))]
    own += [pltpu.make_async_copy(hidden, normed, own_sem.at[2]),
            pltpu.make_async_copy(queries, q_all, own_sem.at[3])]
    for copy in own:
        copy.start()

    barrier = pltpu.get_barrier_semaphore()
    greeted = [{"ctx": (idx + o) % n} for o in range(1, REACH + 1)]
    greeted += [{"ctx": (idx + n - o) % n} for o in range(1, REACH + 1)]
    greeted += [{"ctx": 2 * chip_at((pos + o) % chips) + core} for o in (1, chips - 1)]
    greeted += [{"ctx": sibling}]
    if third:
        greeted += [{"parts": 1 - part}]
    for who in greeted:
        pl.semaphore_signal(barrier, inc=1, device_id=who, device_id_type=MESH)
    pl.semaphore_wait(barrier, len(greeted))

    ways = (0, 1)

    def begin(m):
        for u in (0, 1):
            for d in ways:
                ring(m, d, u, 0, 1).start()
        for d in ways:
            sib_own(m, d, core).start()

    def turn(m, s):
        for u in (0, 1):
            for d in ways:
                ring(m, d, u, s, s).wait_recv()

                @pl.when(s < chips - 1)
                def _():
                    ring(m, d, u, s, s + 1).start()
        for d in ways:
            if third:
                cross(m, d, s, part).start()
            sib(m, d, s, core).start()
        if third:
            @pl.when(s > 1)
            def _():
                for d in ways:
                    cross(m, d, s - 1, 1 - part).wait_recv()
                    cross_sib(m, d, s - 1, core).start()
        if piecewise:
            @pl.when(s > 1)
            def _():
                absorb(m, s - 2)

    def absorb(m, s):
        @pl.when(s == 0)
        def _():
            for d in ways:
                sib_own(m, d, 1 - core).wait_recv()
            acc[m] = jnp.zeros(acc.shape[1:], acc.dtype)

        @pl.when(s > 0)
        def _():
            for d in ways:
                sib(m, d, s, 1 - core).wait_recv()
                if third:
                    cross_sib(m, d, s, 1 - core).wait_recv()

        total = acc[m]
        for d in ways:
            for c in (0, 1):
                start = base(d, s, c)
                total += jnp.dot(
                    normed[:, pl.ds(pl.multiple_of(start, 128), half)], at(m, start, half)[...],
                    preferred_element_type=jnp.float32)
        acc[m] = total

    def last_cross(m):
        if third:
            for d in ways:
                cross(m, d, chips - 1, 1 - part).wait_recv()
                cross_sib(m, d, chips - 1, core).start()

    def gathered(m):
        if piecewise:
            absorb(m, chips - 2)
            absorb(m, chips - 1)
            return
        for d in ways:
            sib_own(m, d, 1 - core).wait_recv()

        @pl.loop(1, chips)
        def _(s):
            for d in ways:
                sib(m, d, s, 1 - core).wait_recv()
                if third:
                    cross_sib(m, d, s, 1 - core).wait_recv()

    def project(m, cols):
        if piecewise:
            return
        step = 1024
        for i in range(depth // step):
            part_sum = jnp.dot(normed[:, i * step:(i + 1) * step],
                               w_all[m, i * step:(i + 1) * step, cols],
                               preferred_element_type=jnp.float32)
            acc[m, :, cols] = part_sum if i == 0 else acc[m, :, cols] + part_sum

    own[0].wait()
    begin(0)
    own[1].wait()
    for o in range(1, blocks):
        @pl.when(idx + o < n)
        def _():
            send_docs(o).start()

        @pl.when(idx < o)
        def _():
            kbuf[o] = jnp.zeros(kbuf.shape[1:], kbuf.dtype)
            vbuf[o] = jnp.zeros(vbuf.shape[1:], vbuf.dtype)
            dbuf[o] = jnp.full(dbuf.shape[1:], -1, dbuf.dtype)
    dbuf[0] = doc[...]
    own[2].wait()

    @pl.loop(0, tok // 16)
    def _(i):
        r16 = pl.ds(pl.multiple_of(i * 16, 16), 16)
        x = normed[r16, :].astype(jnp.float32)
        mean = jnp.sum(x * x, -1, keepdims=True) * (1.0 / depth)
        normed[r16, :] = (x * lax.rsqrt(mean + 1e-05)).astype(jnp.bfloat16)

    own[3].wait()

    @pl.loop(1, chips)
    def _(s):
        turn(0, s)

        @pl.when(s == chips - 4)
        def _():
            begin(1)

        @pl.when(s > chips - 4)
        def _():
            turn(1, s - (chips - 4))

    for o in range(1, blocks):
        @pl.when(idx >= o)
        def _():
            send_docs(o).wait_recv()
    q_docs = jnp.transpose(jnp.broadcast_to(doc[...], (tok, tok)))
    for b in range(blocks):
        allowed = dbuf[b] == q_docs
        if b == 0:
            allowed &= (lax.broadcasted_iota(jnp.int32, (tok, tok), 1)
                        <= lax.broadcasted_iota(jnp.int32, (tok, tok), 0))
        bias[:, b * tok:(b + 1) * tok] = jnp.where(allowed, 0.0, -jnp.inf)

    last_cross(0)
    gathered(0)
    project(0, slice(0, kvw))
    for h in range(KV_HEADS):
        cols = slice(h * HEAD_DIM, (h + 1) * HEAD_DIM)
        x = acc[0, :, cols]
        turned = x * cos2[...] + pltpu.roll(x, HEAD_DIM // 2, 1) * sin2[...]
        kbuf[0, :, cols] = turned.astype(jnp.bfloat16)
    pass_on(0)
    turn(1, 4)
    pass_beside(0)
    turn(1, 5)
    passed(0)

    @pl.loop(6, chips - 2)
    def _(s):
        turn(1, s)

    scale = math.log2(math.e) / math.sqrt(HEAD_DIM)
    per_step = 2

    @pl.loop(0, HEADS // per_step)
    def _(i):
        @pl.when((i % 3 == 0) & (i < 6))
        def _():
            turn(1, chips - 2 + i // 3)

        @pl.when(i == 6)
        def _():
            last_cross(1)

        @pl.when(i == 9)
        def _():
            gathered(1)
            for e in (1, 2):
                cols = groups[e][1]
                project(1, cols)
                vbuf[0, :, cols] = acc[1, :, cols].astype(jnp.bfloat16)
                pass_on(e)

        @pl.when(i == 14)
        def _():
            pass_beside(1)
            pass_beside(2)

        for g in range(per_step):
            h = i * per_step + g
            q = q_all[:, pl.ds(pl.multiple_of(h * HEAD_DIM, HEAD_DIM), HEAD_DIM)]
            k_cols = pl.ds(pl.multiple_of((h // GROUP) * HEAD_DIM, HEAD_DIM), HEAD_DIM)
            k = kbuf[:, :, k_cols].reshape(span, HEAD_DIM)
            scores = lax.dot_general(q, k, (((1,), (1,)), ((), ())),
                                     preferred_element_type=jnp.float32) + bias[...]
            top = jnp.max(scores, -1, keepdims=True)
            expo = jnp.exp2((scores - top) * scale)
            total = jnp.sum(expo, -1, keepdims=True)
            probs[h] = (expo * (1.0 / total)).astype(jnp.bfloat16)

    for e in (1, 2):
        passed(e)

        @pl.loop((e - 1) * HEADS // 2 // per_step, e * HEADS // 2 // per_step)
        def _(i):
            for g in range(per_step):
                h = i * per_step + g
                v_cols = pl.ds(pl.multiple_of((h // GROUP) * HEAD_DIM, HEAD_DIM), HEAD_DIM)
                v = vbuf[:, :, v_cols].reshape(span, HEAD_DIM)
                out[:, pl.ds(pl.multiple_of(h * HEAD_DIM, HEAD_DIM), HEAD_DIM)] = jnp.dot(
                    probs[h], v, preferred_element_type=jnp.float32).astype(jnp.bfloat16)

    for e in range(3):
        for o in (1, 3):
            @pl.when(sibling >= o)
            def _():
                send_beside(e, o).wait_send()
        for o in (2, 4):
            @pl.when(idx + o < n)
            def _():
                send_ahead(e, o).wait_send()
    for o in range(1, blocks):
        @pl.when(idx + o < n)
        def _():
            send_docs(o).wait_send()

    for m in (0, 1):
        for d in ways:
            for u in (0, 1):
                ring(m, d, u, 0, 1).wait_send()
            sib_own(m, d, core).wait_send()

    @pl.loop(1, chips)
    def _(s):
        for m in (0, 1):
            for d in ways:
                @pl.when(s < chips - 1)
                def _():
                    for u in (0, 1):
                        ring(m, d, u, s, s).wait_send()

                sib(m, d, s, core).wait_send()
                if third:
                    cross(m, d, s, part).wait_send()
                    cross_sib(m, d, s, core).wait_send()


def on_device(n, parts, hidden_states, queries, w_key, w_value, doc_ids):
    tok, depth = hidden_states.shape
    kvw = w_key.shape[1]
    half_dim = HEAD_DIM // 2
    place = jnp.arange(HEAD_DIM)
    inverse_freq = 500000.0 ** (-(place % half_dim).astype(jnp.float32) * 2.0 / HEAD_DIM)
    positions = lax.axis_index("ctx") * tok + jnp.arange(tok)
    angles = positions.astype(jnp.float32)[:, None] * inverse_freq[None, :]
    cos2 = jnp.cos(angles)
    sin2 = jnp.sin(angles) * jnp.where(place < half_dim, -1.0, 1.0)[None, :]
    chips = n // 2
    sem = pltpu.SemaphoreType.DMA
    blocks = REACH + 1
    in_vmem = pl.BlockSpec(memory_space=pltpu.VMEM)
    in_any = pl.BlockSpec(memory_space=pl.ANY)
    return pl.pallas_call(
        functools.partial(fused_kernel, n, parts),
        out_shape=jax.ShapeDtypeStruct(queries.shape, jnp.bfloat16),
        in_specs=[in_any, in_any, in_any, in_any, in_vmem, in_vmem, in_vmem],
        out_specs=in_vmem,
        scratch_shapes=[
            pltpu.VMEM((2, depth, kvw), jnp.bfloat16),
            pltpu.VMEM((tok, depth), jnp.bfloat16),
            pltpu.VMEM(queries.shape, jnp.bfloat16),
            pltpu.VMEM((HEADS, tok, blocks * tok), jnp.bfloat16),
            pltpu.VMEM((tok, blocks * tok), jnp.float32),
            pltpu.VMEM((2, tok, kvw), jnp.float32),
            pltpu.VMEM((blocks, tok, kvw), jnp.bfloat16),
            pltpu.VMEM((blocks, tok, kvw), jnp.bfloat16),
            pltpu.VMEM((blocks, 1, tok), jnp.int32),
            sem((4,)),
        ] + [sem((2, 2, 2, chips))] * 2 + [sem((2, 2, chips))] * 6
        + [sem((3, REACH))] * 2 + [sem((REACH,))] * 2,
        compiler_params=pltpu.CompilerParams(
            collective_id=0, has_side_effects=True, vmem_limit_bytes=60 * 2**20),
        name="project_attend",
    )(hidden_states, queries, w_key, w_value, cos2, sin2, doc_ids.reshape(1, tok))


def solution(mesh):
    in_specs = (
        P(("parts", "ctx"), None),
        P(("parts", "ctx"), None),
        P("ctx", None),
        P("ctx", None),
        P(("parts", "ctx")),
    )
    out_specs = P(("parts", "ctx"), None)
    return jax.shard_map(
        functools.partial(on_device, mesh.shape["ctx"], mesh.shape["parts"]),
        mesh=mesh, in_specs=in_specs, out_specs=out_specs, check_vma=False
    )
```
